128 devices in a mesh: narrow: 4 (over y), wide: 32 (over z, x, core).
Axes of the slice: x: 4, y: 4, z: 4, core: 2. Of those that a mesh axis runs over, the one named last changes fastest.
Arguments:
- hidden_state: bfloat16 [256, 8192], P(('narrow', 'wide')), may hold values from -6 to 6
- query_weight: bfloat16 [8192, 8192], P('narrow', 'wide'), may hold values from -0.0625 to 0.0625
- memory_weight: bfloat16 [8192, 2, 1024], P('narrow', None, 'wide'), may hold values from -0.0625 to 0.0625
- output_weight: bfloat16 [8192, 8192], P('wide', 'narrow'), may hold values from -1 to 1
- key_cache: bfloat16 [256, 2048, 1024], P(('narrow', 'wide')), may hold values from -122 to 122
- value_cache: bfloat16 [256, 2048, 1024], P(('narrow', 'wide')), may hold values from -6 to 6
- cache_lengths: int32 [256], P(('narrow', 'wide')), may hold values from 2 to 2048, as said below
Outputs:
- attention_out: bfloat16 [256, 8192], P(('narrow', 'wide'))
The draws below stay inside these ranges and needn't reach their ends.
Inputs may be any that keep to these rules, and one draw needn't show every extreme that they name: `cache_lengths`: each sequence's length; some sequence has exactly 2048.
All inputs are finite; a program needn't handle non-finite values.
Results may differ from the reference program's by a relative error of at most 0.022.
Values may be sent and summed in bfloat16 or wider, within the bound.
No kernel may reach another device: no remote copies, remote signals or barrier semaphores. Data moves between devices by JAX's collectives and lax.ppermute only.
A program may use at most 128 MiB of HBM per device.

```python
import math
import jax
import jax.numpy as jnp
from jax import lax

D = 8192
H = 64
KVH = 8
HD = 128
CACHE = 2048
BATCH = 256


def draw_key_cache(key, part):
    key = jax.random.fold_in(key, 7)
    first_key = jax.random.fold_in(key, 0)
    array_shape = (BATCH, CACHE, KVH * HD)
    drawn_keys = jnp.clip(jax.random.normal(first_key, array_shape, jnp.float32), -6.0, 6.0)
    return drawn_keys.astype(jnp.bfloat16)


def draw_cache_lengths(key, part):
    key = jax.random.fold_in(key, 11)
    cap_key, spot_key, full_key = jax.random.split(key, 3)
    ceiling = jax.random.randint(cap_key, (BATCH,), 2, CACHE + 1)
    spread_bits = jax.random.randint(spot_key, (BATCH,), 0, 1 << 20)
    lengths = 2 + spread_bits % (ceiling - 1)
    chosen = jax.random.randint(full_key, (), 0, BATCH)
    return jnp.where(jnp.arange(BATCH, dtype=jnp.int32) == chosen, CACHE, lengths).astype(jnp.int32)


def level_of(stream_key, shape, shards, smallest, high):
    factor_of, own = 1.0, jax.random.fold_in(stream_key, 6)
    for axis_at, parts in shards:
        draws = jnp.exp(jax.random.uniform(jax.random.fold_in(own, axis_at), (parts,), jnp.float32, smallest / len(shards), high / len(shards)))
        factor_of = factor_of * jnp.repeat(draws, shape[axis_at] // parts).reshape([-1 if axis == axis_at else 1 for axis in range(len(shape))])
    return factor_of


def noise(stream_key, dims, width, reach, cuts=(), kind=jnp.bfloat16):
    factor_of = level_of(stream_key, dims, cuts, -0.22, 0.18) if cuts else 1.0
    entries = jax.random.normal(stream_key, dims, jnp.float32) * width * factor_of
    return jnp.minimum(jnp.maximum(entries, -reach), reach).astype(kind)


def setup_inputs(seed: int = 0) -> dict:
    streams_of = jax.random.split(jax.random.key(seed), 8)
    return {
        "hidden_state": noise(streams_of[0], (BATCH, D), 1.0, 6.0, ((0, 128),)),
        "query_weight": noise(streams_of[1], (D, H * HD), D ** -0.5, 0.0625, ((0, 4), (1, 32))),
        "memory_weight": noise(streams_of[2], (D, 2, KVH * HD), D ** -0.5, 0.0625, ((0, 4), (2, 32))),
        "output_weight": noise(streams_of[3], (H * HD, D), (HD // 4) ** -0.5, 1.0, ((0, 32), (1, 4))),
        "key_cache": draw_key_cache(jax.random.fold_in(streams_of[7], 71), 0),
        "value_cache": noise(streams_of[5], (BATCH, CACHE, KVH * HD), 1.0, 6.0, ((0, 128),)),
        "cache_lengths": draw_cache_lengths(jax.random.fold_in(streams_of[7], 71), 0),
    }


rope_base = 500000.0
masked_score = -1e+30

def rotate(values, positions):
    half_width = values.shape[-1] // 2
    frequency = jnp.exp(-jnp.log(rope_base) * jnp.arange(half_width, dtype=jnp.float32) * 2.0 / values.shape[-1])
    angles = positions.astype(jnp.float32)[:, None, None] * frequency
    cosine = jnp.cos(angles)
    sine_part = jnp.sin(angles)
    first_half = values[..., :half_width]
    second = values[..., half_width:]
    return jnp.concatenate([first_half * cosine - second * sine_part, second * cosine + first_half * sine_part], axis=-1)

def reference(hidden_state, query_weight, memory_weight, output_weight, key_cache, value_cache, cache_lengths):
    score_scale = 1.0 / math.sqrt(HD)
    queries = jnp.dot(hidden_state, query_weight, preferred_element_type=jnp.float32).astype(jnp.bfloat16)
    fresh = jnp.dot(hidden_state, memory_weight.reshape(D, 2 * KVH * HD), preferred_element_type=jnp.float32).astype(jnp.bfloat16)
    fresh_keys = fresh[:, :KVH * HD].reshape(-1, KVH, HD)
    fresh_values = fresh[:, KVH * HD:].reshape(-1, KVH, HD)
    rotated_queries = rotate(queries.astype(jnp.float32).reshape(-1, H, HD), cache_lengths).astype(jnp.bfloat16)
    rotated_keys = rotate(fresh_keys.astype(jnp.float32), cache_lengths).astype(jnp.bfloat16)

    def single_row(inputs):
        query_row, key_row, value_row, cached_keys, cached_values, length = inputs
        grouped = query_row.astype(jnp.float32).reshape(KVH, H // KVH, HD)
        key_block = cached_keys.astype(jnp.float32).reshape(CACHE, KVH, HD)
        scores = jnp.einsum('gjd,sgd->gjs', grouped, key_block) * score_scale
        live_mask = jnp.arange(CACHE, dtype=jnp.int32) < length
        scores = jnp.where(live_mask, scores, masked_score)
        own_score = jnp.einsum('gjd,gd->gj', grouped, key_row.astype(jnp.float32)) * score_scale
        everyone = jnp.concatenate([scores, own_score[..., None]], axis=-1)
        row_max = lax.optimization_barrier(jnp.max(everyone, axis=-1, keepdims=True))
        exps = jnp.exp(everyone - row_max)
        denominator = lax.optimization_barrier(jnp.sum(exps, axis=-1))
        rounded = lax.optimization_barrier(exps.astype(jnp.bfloat16))
        weights = rounded.astype(jnp.float32)
        value_block = jnp.concatenate([cached_values.astype(jnp.float32).reshape(CACHE, KVH, HD), value_row.astype(jnp.float32)[None]], axis=0)
        mixed = jnp.einsum('gjs,sgd->gjd', weights, value_block) / denominator[..., None]
        return mixed.reshape(H * HD)
    attended = lax.map(single_row, (rotated_queries, rotated_keys, fresh_values, key_cache, value_cache, cache_lengths)).astype(jnp.bfloat16)
    return jnp.dot(attended, output_weight, preferred_element_type=jnp.float32).astype(jnp.bfloat16)
```

```python
import math

import jax
import jax.numpy as jnp
from jax import lax
from jax.experimental import pallas as pl
from jax.experimental.pallas import tpu as pltpu
from jax.sharding import Mesh
from jax.sharding import PartitionSpec as P

HD = 128
KVH = 8
PER = 8
ROPE_BASE = 500000.0
MASKED = -1e30
BLOCK = 512
MIB = 1024 * 1024

HIDE_WEIGHTS = pl.CostEstimate(flops=6 * 10**9, bytes_accessed=2**20, transcendentals=0)
HIDE_CACHES = pl.CostEstimate(flops=3 * 10**10, bytes_accessed=2**21, transcendentals=0)

CHIPS = ("y", "z", "x")
ALL = ("y", "z", "x", "c")
CORE_FIRST = ("c", "y", "z", "x")

VMEM = pl.BlockSpec(memory_space=pltpu.VMEM)
SMEM = pl.BlockSpec(memory_space=pltpu.SMEM)


def rope_tables(positions):
    half = HD // 2
    frequency = jnp.exp(
        -jnp.log(ROPE_BASE) * jnp.arange(half, dtype=jnp.float32) * 2.0 / HD
    )
    angles = positions.astype(jnp.float32)[:, None] * frequency
    cosine = jnp.cos(angles)
    sine = jnp.sin(angles)
    return (
        jnp.concatenate([cosine, cosine], axis=-1),
        jnp.concatenate([-sine, sine], axis=-1),
    )


def flat(block):
    return block.reshape((block.shape[0] * block.shape[1], block.shape[2]))


def stage_kernel(hidden_ref, o_ref):
    o_ref[...] = hidden_ref[...]


def stage_hidden(hidden):
    return pl.pallas_call(
        stage_kernel,
        out_shape=jax.ShapeDtypeStruct(hidden.shape, hidden.dtype),
        in_specs=[VMEM],
        out_specs=VMEM,
        compiler_params=pltpu.CompilerParams(vmem_limit_bytes=8 * MIB),
        name="stage_hidden",
    )(hidden)


def spread_kernel(hidden_ref, o_ref):
    narrow, plane, _, part = o_ref.shape
    for y in range(narrow):
        piece = hidden_ref[:, y * part : (y + 1) * part]
        for i in range(plane):
            o_ref[y, i] = piece


def spread_hidden(hidden, narrow, plane):
    rows, model = hidden.shape
    return pl.pallas_call(
        spread_kernel,
        out_shape=jax.ShapeDtypeStruct((narrow, plane, rows, model // narrow), hidden.dtype),
        in_specs=[VMEM],
        out_specs=VMEM,
        compiler_params=pltpu.CompilerParams(vmem_limit_bytes=8 * MIB),
        cost_estimate=HIDE_WEIGHTS,
        name="spread_hidden",
    )(hidden)


def multiply(tokens_ref, query_ref, memory_ref):
    tokens = flat(tokens_ref[...])
    queries = jnp.dot(tokens, query_ref[...], preferred_element_type=jnp.float32)
    memory = lax.dot_general(
        tokens,
        memory_ref[...],
        (((1,), (1,)), ((), ())),
        preferred_element_type=jnp.float32,
    )
    return jnp.concatenate([queries.astype(jnp.bfloat16), memory.astype(jnp.bfloat16)], axis=1)


def project_mine_kernel(tokens_ref, query_ref, memory_ref, o_ref):
    o_ref[...] = multiply(tokens_ref, query_ref, memory_ref).reshape(o_ref.shape)


def project_other_kernel(tokens_ref, mine_ref, query_ref, memory_ref, o_ref):
    core = lax.axis_index("c")
    o_ref[core] = mine_ref[...]
    o_ref[1 - core] = multiply(tokens_ref, query_ref, memory_ref).reshape(o_ref.shape[1:])


def project_mine(tokens, query_weight, memory_weight):
    chips, rows, part = tokens.shape
    cols = query_weight.shape[1] + memory_weight.shape[0]
    return pl.pallas_call(
        project_mine_kernel,
        out_shape=jax.ShapeDtypeStruct((chips, rows, cols), jnp.bfloat16),
        in_specs=[VMEM] * 3,
        out_specs=VMEM,
        compiler_params=pltpu.CompilerParams(vmem_limit_bytes=12 * MIB),
        cost_estimate=pl.CostEstimate(flops=10**9, bytes_accessed=2**20, transcendentals=0),
        name="project_mine",
    )(tokens, query_weight, memory_weight)


def project_other(tokens, mine, query_weight, memory_weight):
    return pl.pallas_call(
        project_other_kernel,
        out_shape=jax.ShapeDtypeStruct((2,) + mine.shape, jnp.bfloat16),
        in_specs=[VMEM] * 4,
        out_specs=VMEM,
        compiler_params=pltpu.CompilerParams(vmem_limit_bytes=12 * MIB),
        cost_estimate=HIDE_CACHES,
        name="project_other",
    )(tokens, mine, query_weight, memory_weight)


def attend_kernel(
    lengths_ref, cosine_ref, sine_ref, part_ref, k_ref, v_ref, o_ref,
    sums, queries, fresh_keys, fresh_values, scores, attended, paired,
):
    rows, cache, _ = k_ref.shape
    narrow, plane = part_ref.shape[1:3]
    scale = 1.0 / math.sqrt(HD)
    pair = 2 * PER
    span = plane * rows

    for c in range(2):
        total = flat(part_ref[c, 0]).astype(jnp.float32)
        for y in range(1, narrow):
            total += flat(part_ref[c, y]).astype(jnp.float32)
        total = total.astype(jnp.bfloat16).astype(jnp.float32)
        for j in range(2):
            sums[j, c * span : (c + 1) * span] = total[:, j * HD : (j + 1) * HD]
        sums[2, c * span : (c + 1) * span, : HD // 2] = total[:, 2 * HD :]

    lane = lax.broadcasted_iota(jnp.int32, (KVH, HD), 1) // 32
    for s in range(rows):
        cosine = cosine_ref[s : s + 1]
        sine = sine_ref[s : s + 1]

        def rotate(block):
            return block * cosine + pltpu.roll(block, HD // 2, 1) * sine

        for c in range(2):
            for j in range(2):
                piece = sums[j, pl.ds(c * span + s, plane, stride=rows), :]
                queries[s, pl.ds(2 * c + j, plane, stride=4), :] = rotate(piece)
        key = jnp.zeros((KVH, HD), jnp.float32)
        value = jnp.zeros((KVH, HD), jnp.float32)
        for b in range(2):
            for c in range(2):
                m = 2 * b + c
                piece = sums[2, pl.ds(c * span + b * rows + s, KVH, stride=2 * rows), :]
                key = jnp.where(lane == m, pltpu.roll(piece, 32 * m, 1) if m else piece, key)
                value = jnp.where(
                    lane == m, pltpu.roll(piece, (32 * m - 32) % HD, 1) if m != 1 else piece, value
                )
        fresh_keys[s] = rotate(key).astype(jnp.bfloat16).astype(jnp.float32)
        fresh_values[s] = value

    def spread_groups(block):
        return jnp.concatenate(
            [jnp.broadcast_to(block[g : g + 1], (PER, HD)) for g in range(KVH)], axis=0
        )

    @pl.loop(0, rows)
    def _(s):
        length = lengths_ref[s]
        halves = (length + (BLOCK - 1)) // BLOCK
        whole = halves // 2
        rest = halves - 2 * whole
        q = queries[s].astype(jnp.bfloat16)
        blank = jnp.zeros((PER, HD), jnp.bfloat16)
        wide_q = []
        for t in range(KVH // 2):
            lower = q[t * pair : t * pair + PER]
            upper = q[t * pair + PER : (t + 1) * pair]
            wide_q.append(
                jnp.concatenate(
                    [
                        jnp.concatenate([lower, blank], axis=1),
                        jnp.concatenate([blank, upper], axis=1),
                    ],
                    axis=0,
                )
            )
        own = (
            jnp.sum(q.astype(jnp.float32) * spread_groups(fresh_keys[s]), axis=1, keepdims=True)
            * scale
        )

        def score(start, size, top):
            at = pl.ds(pl.multiple_of(start, BLOCK), size)
            block = (
                jnp.concatenate(
                    [
                        lax.dot_general(
                            wide_q[t],
                            k_ref[s, at, 2 * t * HD : 2 * (t + 1) * HD],
                            (((1,), (1,)), ((), ())),
                            preferred_element_type=jnp.float32,
                        )
                        for t in range(KVH // 2)
                    ],
                    axis=0,
                )
                * scale
            )
            position = start + lax.broadcasted_iota(jnp.int32, block.shape, 1)
            block = jnp.where(position < length, block, MASKED)
            scores[:, at] = block
            return jnp.maximum(top, jnp.max(block, axis=1, keepdims=True))

        top = lax.fori_loop(0, whole, lambda i, c: score(2 * i * BLOCK, 2 * BLOCK, c), own)
        top = lax.fori_loop(0, rest, lambda i, c: score(2 * whole * BLOCK, BLOCK, c), top)
        own_exp = jnp.exp(own - top)

        def mix(start, size, carry):
            total, mixed = carry
            at = pl.ds(pl.multiple_of(start, BLOCK), size)
            exps = jnp.exp(scores[:, at] - top)
            weights = exps.astype(jnp.bfloat16)
            parts = []
            for t in range(KVH // 2):
                both = jnp.dot(
                    weights[t * pair : (t + 1) * pair],
                    v_ref[s, at, 2 * t * HD : 2 * (t + 1) * HD],
                    preferred_element_type=jnp.float32,
                )
                parts += [both[:PER, :HD], both[PER:, HD:]]
            return (
                total + jnp.sum(exps, axis=1, keepdims=True),
                mixed + jnp.concatenate(parts, axis=0),
            )

        carry = (
            own_exp,
            own_exp.astype(jnp.bfloat16).astype(jnp.float32) * spread_groups(fresh_values[s]),
        )
        carry = lax.fori_loop(0, whole, lambda i, c: mix(2 * i * BLOCK, 2 * BLOCK, c), carry)
        total, mixed = lax.fori_loop(0, rest, lambda i, c: mix(2 * whole * BLOCK, BLOCK, c), carry)
        attended[s] = mixed / total

    for s in range(rows):
        for h in range(4):
            paired[h, pl.ds(s, plane, stride=rows), :] = attended[
                s, pl.ds(h, plane, stride=4), :
            ]
    block = jnp.concatenate([paired[h] for h in range(4)], axis=1).astype(jnp.bfloat16)
    block = block.reshape(o_ref.shape[1:])
    for y in range(narrow):
        o_ref[y] = block


def attend(partial, cosine, sine, key_cache, value_cache, lengths):
    _, narrow, plane, rows, cols = partial.shape
    cache, width = key_cache.shape[1:]
    heads = 4 * plane
    return pl.pallas_call(
        attend_kernel,
        out_shape=jax.ShapeDtypeStruct((narrow, plane, rows, 4 * HD), jnp.bfloat16),
        in_specs=[SMEM] + [VMEM] * 5,
        out_specs=VMEM,
        scratch_shapes=[
            pltpu.VMEM((3, 2 * plane * rows, HD), jnp.float32),
            pltpu.VMEM((rows, heads, HD), jnp.float32),
            pltpu.VMEM((rows, KVH, HD), jnp.float32),
            pltpu.VMEM((rows, KVH, HD), jnp.float32),
            pltpu.VMEM((heads, cache), jnp.float32),
            pltpu.VMEM((rows, heads, HD), jnp.float32),
            pltpu.VMEM((4, plane * rows, HD), jnp.float32),
        ],
        compiler_params=pltpu.CompilerParams(vmem_limit_bytes=24 * MIB),
        cost_estimate=pl.CostEstimate(
            flops=8 * rows * heads * cache * HD,
            bytes_accessed=4 * rows * cache * width,
            transcendentals=rows * heads * cache,
        ),
        name="attend",
    )(lengths, cosine, sine, partial, key_cache, value_cache)


def output_kernel(tokens_ref, weight_ref, other_ref, o_ref):
    core = lax.axis_index("c")
    heads = weight_ref.shape[0]

    def half(owner, ref):
        at = pl.ds(pl.multiple_of(owner * heads, heads), heads)
        return jnp.dot(
            flat(tokens_ref[:, :, at]), ref[...], preferred_element_type=jnp.float32
        )

    total = half(core, weight_ref) + half(1 - core, other_ref)
    o_ref[...] = total.astype(jnp.bfloat16).reshape(o_ref.shape)


def output(tokens, weight, other):
    chips, rows, _ = tokens.shape
    return pl.pallas_call(
        output_kernel,
        out_shape=jax.ShapeDtypeStruct((chips, rows, weight.shape[1]), jnp.bfloat16),
        in_specs=[VMEM] * 3,
        out_specs=VMEM,
        compiler_params=pltpu.CompilerParams(vmem_limit_bytes=12 * MIB),
        name="output",
    )(tokens, weight, other)


def gather_sums_kernel(parts_ref, o_ref):
    narrow, plane, rows, part = parts_ref.shape
    span = plane * rows
    pick = lax.broadcasted_iota(jnp.int32, (PER, span), 1) % rows
    pick = (pick == lax.broadcasted_iota(jnp.int32, (PER, span), 0)).astype(jnp.bfloat16)
    for y in range(narrow):
        total = jnp.dot(pick, flat(parts_ref[y]), preferred_element_type=jnp.float32)
        o_ref[:, y * part : (y + 1) * part] = total[:rows].astype(o_ref.dtype)


def gather_sums(parts):
    narrow, plane, rows, part = parts.shape
    return pl.pallas_call(
        gather_sums_kernel,
        out_shape=jax.ShapeDtypeStruct((rows, narrow * part), jnp.bfloat16),
        in_specs=[VMEM],
        out_specs=VMEM,
        compiler_params=pltpu.CompilerParams(vmem_limit_bytes=8 * MIB),
        name="gather_sums",
    )(parts)


def on_device(
    hidden_state, query_weight, memory_weight, output_weight, key_cache, value_cache, cache_lengths
):
    narrow = lax.axis_size("y")
    plane = lax.axis_size("z") * lax.axis_size("x")
    chips = narrow * plane
    swap = [(0, 1), (1, 0)]
    rows, model = hidden_state.shape
    part = model // narrow
    query_cols = query_weight.shape[1]
    cols = query_cols + 2 * memory_weight.shape[2]
    heads_local = output_weight.shape[0]

    pieces = spread_hidden(stage_hidden(hidden_state), narrow, plane).reshape(chips, rows, part)
    mine = lax.all_to_all(pieces, CHIPS, split_axis=0, concat_axis=0, tiled=True)
    mine, lengths = lax.optimization_barrier((mine, cache_lengths))
    other = lax.ppermute(mine, "c", swap)
    tables = rope_tables(lengths)
    memory_weight = memory_weight.transpose(1, 2, 0).reshape(-1, part)
    from_mine = project_mine(mine, query_weight, memory_weight)
    other, from_mine, cosine, sine, own_output = lax.optimization_barrier(
        (other, from_mine, *tables, output_weight)
    )
    other_output = lax.ppermute(own_output, "c", swap)

    partial = project_other(other, from_mine, query_weight, memory_weight)
    partial = lax.all_to_all(
        partial.reshape(2 * chips, rows, cols), CORE_FIRST, split_axis=0, concat_axis=0, tiled=True
    )

    spread = attend(
        partial.reshape(2, narrow, plane, rows, cols),
        cosine,
        sine,
        key_cache,
        value_cache,
        lengths,
    )
    spread, other_output = lax.optimization_barrier((spread, other_output))

    gathered = lax.all_to_all(
        spread.reshape(chips, rows, 2 * heads_local),
        CHIPS,
        split_axis=0,
        concat_axis=0,
        tiled=True,
    )
    summed = output(gathered, own_output, other_output)
    returned = lax.all_to_all(summed, CHIPS, split_axis=0, concat_axis=0, tiled=True)
    return gather_sums(returned.reshape(narrow, plane, rows, part))


def solution(mesh):
    count = mesh.devices.size
    narrow = mesh.shape["narrow"]
    side = math.isqrt(mesh.shape["wide"] // 2)
    split = Mesh(mesh.devices.reshape(narrow, side, count // (2 * narrow * side), 2), ALL)
    wide = ("z", "x", "c")
    in_specs = (
        P(ALL, None),
        P("y", wide),
        P("y", None, wide),
        P(wide, "y"),
        P(ALL, None, None),
        P(ALL, None, None),
        P(ALL),
    )
    return jax.shard_map(
        on_device, mesh=split, in_specs=in_specs, out_specs=P(ALL, None), check_vma=False
    )
```
